256 devices in a mesh: rows: 64 (over x, z, core), grp: 4 (over y).
Axes of the slice: x: 4, y: 4, z: 8, core: 2. Of those that a mesh axis runs over, the one named last changes fastest.
Arguments:
- table: bfloat16 [524288, 512], P(('rows', 'grp')), may hold values from -30 to 30
- sketch: bfloat16 [512, 256], replicated, may hold values from -0.25 to 0.25
Outputs:
- basis: float32 [524288, 256], P(('rows', 'grp'))
- projection: float32 [256, 512], replicated
The draws below stay inside these ranges and needn't reach their ends.
All inputs are finite; a program needn't handle non-finite values.
Results may differ from the reference program's by a relative error of at most 0.0004.
Values sent between devices are 32-bit elements; how exact they have to be, the bound alone decides.
No kernel may reach another device: no remote copies, remote signals or barrier semaphores. Data moves between devices by JAX's collectives and lax.ppermute only.
A program may use at most 64 MiB of HBM per device.

```python
import math
import jax
import jax.numpy as jnp
from jax import lax

N = 512
K = 256
SWEEPS = 12
TOTAL_ROWS = 524288


def draw_table(key, part):
    key = jax.random.fold_in(key, 11)
    key_col, key_row, key_ent = jax.random.split(key, 3)
    rise = jnp.exp(jnp.log(3.0) * jnp.arange(TOTAL_ROWS, dtype=jnp.float32) / TOTAL_ROWS)
    row_scale = jnp.exp(jax.random.uniform(key_row, (TOTAL_ROWS, 1), jnp.float32, jnp.log(0.2), jnp.log(2.0)))
    entries = jnp.clip(jax.random.normal(key_ent, (TOTAL_ROWS, N), jnp.float32), -5.0, 5.0)
    col_scale = jnp.exp(jax.random.uniform(key_col, (N,), jnp.float32, jnp.log(0.1), 0.0))
    values = entries * col_scale[None, :] * row_scale * rise[:, None]
    return values.astype(jnp.bfloat16)


def gaussian(key, shape, spread, reach, kind=jnp.bfloat16):
    drawn = spread * jax.random.normal(key, shape, jnp.float32)
    return jnp.clip(drawn, min=-reach, max=reach).astype(kind)


def setup_inputs(seed: int = 0) -> dict:
    arg_keys = jax.random.split(jax.random.key(seed), 3)
    table = draw_table(jax.random.fold_in(arg_keys[2], 71), 0)
    sketch = gaussian(arg_keys[1], (N, K), N ** -0.5, 0.25)
    return {"table": table, "sketch": sketch}


def inverse_root(gram):
    high = lax.Precision.HIGHEST
    eye = jnp.eye(gram.shape[0], dtype=jnp.float32)
    scale = jnp.sqrt(jnp.sum(gram * gram))
    start_y = gram / scale

    def sweep(index, carry):
        cur_y, cur_z = carry
        factor = 1.5 * eye - 0.5 * jnp.dot(cur_z, cur_y, precision=high)
        return (jnp.dot(cur_y, factor, precision=high), jnp.dot(factor, cur_z, precision=high))
    final_y, final_z = lax.fori_loop(0, SWEEPS, sweep, (start_y, eye))
    return final_z / jnp.sqrt(scale)

def reference(table, sketch):
    high = lax.Precision.HIGHEST
    wide_table = table.astype(jnp.float32)
    first_range = jnp.dot(table, sketch, preferred_element_type=jnp.float32)
    first_gram = jnp.einsum('rk,rl->kl', first_range, first_range, precision=high)
    first_inverse = inverse_root(first_gram)
    first_basis = jnp.dot(first_range, first_inverse, precision=high)
    power = jnp.einsum('rn,rk->nk', wide_table, first_basis, precision=high)
    second_range = jnp.dot(wide_table, power, precision=high)
    second_gram = jnp.einsum('rk,rl->kl', second_range, second_range, precision=high)
    second_inverse = inverse_root(second_gram)
    second_basis = jnp.dot(second_range, second_inverse, precision=high)
    root = math.sqrt(TOTAL_ROWS)
    basis = second_basis * root
    coeff = jnp.einsum('rk,rn->kn', second_basis, wide_table, precision=high)
    return (basis, coeff / root)
```

```python
import functools
import math

import jax
import jax.numpy as jnp
from jax import lax
from jax.experimental import pallas as pl
from jax.experimental.pallas import tpu as pltpu
from jax.sharding import Mesh, PartitionSpec as P

SWEEPS = 12
BLOCK = 256
F32 = jnp.float32
BF16 = jnp.bfloat16


def dot(a, b):
    return jnp.dot(a, b, preferred_element_type=F32)


def split2(x):
    high = x.astype(BF16)
    return high, (x - high.astype(F32)).astype(BF16)


def split3(x):
    high = x.astype(BF16)
    rest = x - high.astype(F32)
    mid = rest.astype(BF16)
    return high, mid, (rest - mid.astype(F32)).astype(BF16)


def times(a, b):
    if len(a) == 3 and len(b) == 3:
        low = dot(a[0], b[2]) + dot(a[1], b[1]) + dot(a[2], b[0])
        return low + (dot(a[0], b[1]) + dot(a[1], b[0])) + dot(a[0], b[0])
    total = None
    for part in reversed(a):
        for other in reversed(b):
            term = dot(part, other)
            total = term if total is None else total + term
    return total


def inverse_root(gram):
    n = gram.shape[0]
    scale = jnp.sqrt(jnp.sum(gram * gram))
    eye = lax.broadcasted_iota(jnp.int32, (n, n), 0) == lax.broadcasted_iota(jnp.int32, (n, n), 1)

    def advance(w, parts):
        square = times(parts, parts)
        return 2.25 * w - 1.5 * square + 0.25 * times(split2(square), parts)

    def sweep(index, carry):
        w, z = carry
        parts = split2(w)
        return advance(w, parts), 1.5 * z - 0.5 * times(split2(z), parts)

    w = gram * (1.0 / scale)
    z = jnp.where(eye, 1.5, 0.0) - 0.5 * w
    w = advance(w, split2(w))
    w, z = lax.fori_loop(0, SWEEPS - 2, sweep, (w, z))
    z = 1.5 * z - 0.5 * times(split2(z), split2(w))
    return z * (1.0 / jnp.sqrt(scale))


def finish(size, total_ref, sketch_ref, table_hbm, basis_hbm, coeff_ref, table, basis, in_sem, out_sem):
    fetch = pltpu.make_async_copy(table_hbm, table, in_sem)
    fetch.start()
    k = sketch_ref.shape[1]
    corner = total_ref[k : 2 * k, :]
    upper = jnp.concatenate([total_ref[0:k, :], corner], 1)
    lower = jnp.concatenate([corner.T, total_ref[2 * k : 3 * k, :]], 1)
    total = split3(jnp.concatenate([upper, lower], 0))
    sketch = sketch_ref[...]
    sketch_t = sketch.astype(F32).T.astype(BF16)
    first = split3(times(total, (sketch,)))
    first_inverse = inverse_root(times((sketch_t,), first))
    power = times(first, split3(first_inverse))
    power_parts = split3(power)
    table_power = split3(times(total, power_parts))
    second_inverse = split3(inverse_root(times(split3(power.T), table_power)))
    weight = split3(times(power_parts, second_inverse) * size)
    fetch.wait()
    copies = []
    for index in range(table.shape[0] // BLOCK):
        rows = pl.ds(index * BLOCK, BLOCK)
        basis[rows, :] = times((table[rows, :],), weight)
        copy = pltpu.make_async_copy(basis.at[rows], basis_hbm.at[rows], out_sem.at[index])
        copy.start()
        copies.append(copy)
    coeff_ref[...] = times(table_power, second_inverse).T * (1.0 / size)
    for copy in copies:
        copy.wait()


def finish_call(size, total, sketch, table):
    rows, n = table.shape
    k = sketch.shape[1]
    vmem = pl.BlockSpec(memory_space=pltpu.VMEM)
    hbm = pl.BlockSpec(memory_space=pl.ANY)
    return pl.pallas_call(
        functools.partial(finish, size),
        out_shape=(jax.ShapeDtypeStruct((rows, k), F32), jax.ShapeDtypeStruct((k, n), F32)),
        in_specs=[vmem, vmem, hbm],
        out_specs=(hbm, vmem),
        scratch_shapes=[
            pltpu.VMEM((rows, n), BF16),
            pltpu.VMEM((rows, k), F32),
            pltpu.SemaphoreType.DMA,
            pltpu.SemaphoreType.DMA((rows // BLOCK,)),
        ],
        compiler_params=pltpu.CompilerParams(vmem_limit_bytes=48 * 2**20),
    )(total, sketch, table)


def scatter_sum(block, axes):
    return jnp.sum(lax.all_to_all(block, axes, 0, 0), 0)


def gather(block, axes):
    count = lax.axis_size(axes)
    copies = jnp.broadcast_to(block[None], (count,) + block.shape)
    return lax.all_to_all(copies, axes, 0, 0)


def summed(local):
    plane = ("x", "y")
    core = lax.axis_index("core")
    swap = [(0, 1), (1, 0)]
    halves = local.reshape((2, -1) + local.shape[1:])
    keep = lax.dynamic_index_in_dim(halves, core, 0, False)
    send = lax.dynamic_index_in_dim(halves, 1 - core, 0, False)
    half = keep + lax.ppermute(send, "core", swap)
    part = scatter_sum(half.reshape((lax.axis_size(plane), -1) + half.shape[1:]), plane)
    part = jnp.sum(gather(part, "z"), 0)
    half = gather(part, plane).reshape(half.shape)
    other = lax.ppermute(half, "core", swap)
    first = jnp.where(core == 0, half, other)
    second = jnp.where(core == 0, other, half)
    return jnp.concatenate([first, second], 0)


def on_device(table, sketch):
    k = sketch.shape[1]
    count = table.shape[0] * lax.axis_size(("x", "z", "core", "y"))
    left, right = table[:, :k], table[:, k:]

    def gram(a, b):
        return jnp.einsum("rn,rm->nm", a, b, preferred_element_type=F32)

    local = jnp.concatenate([gram(left, left), gram(left, right), gram(right, right)], 0)
    return finish_call(math.sqrt(count), summed(local), sketch, table)


def solution(mesh):
    fine = Mesh(mesh.devices.reshape(4, 8, 2, 4), ("x", "z", "core", "y"))
    split = P(("x", "z", "core", "y"), None)
    return jax.shard_map(
        on_device, mesh=fine, in_specs=(split, P()), out_specs=(split, P()), check_vma=False
    )
```

```python
import functools
import math

import jax
import jax.numpy as jnp
from jax import lax
from jax.experimental import pallas as pl
from jax.experimental.pallas import tpu as pltpu
from jax.sharding import Mesh, PartitionSpec as P

SWEEPS = 12
NEAR = 8
BLOCK = 256
TILE = 128
PAIRS = [(i, j) for i in range(4) for j in range(i, 4)]
HALF = len(PAIRS) // 2 * TILE
F32 = jnp.float32
BF16 = jnp.bfloat16
VMEM = pl.BlockSpec(memory_space=pltpu.VMEM)
HBM = pl.BlockSpec(memory_space=pl.ANY)
PARAMS = pltpu.CompilerParams(vmem_limit_bytes=48 * 2**20)


def dot(a, b):
    return jnp.dot(a, b, preferred_element_type=F32)


def split(x):
    high = x.astype(BF16)
    return high, (x - high.astype(F32)).astype(BF16)


def times(a, b):
    total = None
    for part in reversed(a):
        for other in reversed(b):
            term = dot(part, other)
            total = term if total is None else total + term
    return total


def product(a, b, low):
    half = a[0].shape[0] // 2
    out = []
    for start in (0, half):
        high = a[0][start : start + half]
        rest = a[1][start : start + half]
        both = jnp.concatenate([high, rest], 0)
        large = dot(both, b[0])
        small = dot(both if low else high, b[1])
        sums = small[:half] + large[half:]
        if low:
            sums = small[half:] + sums
        out.append(sums + large[:half])
    return jnp.concatenate(out, 0)


def inverse_root(gram):
    n = gram.shape[0]
    scale = jnp.sqrt(jnp.sum(gram * gram))
    eye = lax.broadcasted_iota(jnp.int32, (n, n), 0) == lax.broadcasted_iota(jnp.int32, (n, n), 1)

    def far(index, carry):
        w, z = carry
        parts = split(w)
        square = product(parts, parts, True)
        z = 1.5 * z - 0.5 * product(split(z), parts, False)
        cube = product(split(square), parts, False)
        return 2.25 * w - 1.5 * square + 0.25 * cube, z

    def near(index, carry):
        e, z = carry
        parts = split(e)
        square = product(parts, parts, False)
        z = z + product(split(z), parts, False)
        return 1.5 * square + product(split(square), parts, False), z

    w = gram * (1.0 / scale)
    z = jnp.where(eye, 1.5, 0.0) - 0.5 * w
    parts = split(w)
    square = product(parts, parts, True)
    w = 2.25 * w - 1.5 * square + 0.25 * product(split(square), parts, False)
    w, z = lax.fori_loop(1, NEAR, far, (w, z))
    e = jnp.where(eye, 0.5, 0.0) - 0.5 * w
    e, z = lax.fori_loop(NEAR, SWEEPS - 1, near, (e, z))
    z = z + product(split(z), split(e), False)
    return z * (1.0 / jnp.sqrt(scale))


def gram_kernel(table_ref, keep_ref, send_ref):
    table = table_ref[...]
    k = table.shape[1] // 2

    def gram(a, b):
        return lax.dot_general(a, b, (((0,), (0,)), ((), ())), preferred_element_type=F32)

    upper = gram(table[:, :k], table)
    lower = gram(table[:, k:], table[:, k:])
    tiles = []
    for i, j in PAIRS:
        source, row, col = (upper, i, j) if i < 2 else (lower, i - 2, j - 2)
        tiles.append(source[row * TILE : (row + 1) * TILE, col * TILE : (col + 1) * TILE])
    count = len(PAIRS) // 2
    core = lax.axis_index("core")

    def store(mine, others):
        for n in range(count):
            rows = pl.ds(n * TILE, TILE)
            keep_ref[rows, :] = mine[n]
            send_ref[rows, :] = others[n]

    @pl.when(core == 0)
    def _():
        store(tiles[:count], tiles[count:])

    @pl.when(core != 0)
    def _():
        store(tiles[count:], tiles[:count])


def gram_call(table):
    half = jax.ShapeDtypeStruct((HALF, TILE), F32)
    return pl.pallas_call(
        gram_kernel,
        out_shape=(half, half),
        in_specs=[VMEM],
        out_specs=(VMEM, VMEM),
        compiler_params=PARAMS,
    )(table)


def finish(size, mine_ref, other_ref, sketch_ref, table_hbm, basis_hbm, coeff_hbm, table, basis, coeff, in_sem, out_sem):
    fetch = pltpu.make_async_copy(table_hbm, table, in_sem)
    fetch.start()
    first_core = lax.axis_index("core") == 0
    mine, other = mine_ref[...], other_ref[...]
    tiles = {}
    for n, half in enumerate((jnp.where(first_core, mine, other), jnp.where(first_core, other, mine))):
        for m in range(HALF // TILE):
            i, j = PAIRS[n * (HALF // TILE) + m]
            tile = half[m * TILE : (m + 1) * TILE, :]
            tiles[i, j] = tile
            if i != j:
                tiles[j, i] = tile.T
    total = split(jnp.concatenate([jnp.concatenate([tiles[i, j] for j in range(4)], 1) for i in range(4)], 0))
    sketch = sketch_ref[...]
    first = split(times(total, (sketch,)))
    power = times(first, split(inverse_root(times((sketch.astype(F32).T.astype(BF16),), first))))
    parts = split(power)
    table_power = split(times(total, parts))
    second_inverse = split(inverse_root(times(split(power.T), table_power)))
    weight = split(times(parts, second_inverse) * size)
    fetch.wait()
    copies = []
    blocks = table.shape[0] // BLOCK
    for index in range(blocks):
        rows = pl.ds(index * BLOCK, BLOCK)
        basis[rows, :] = times((table[rows, :],), weight)
        copy = pltpu.make_async_copy(basis.at[rows], basis_hbm.at[rows], out_sem.at[index])
        copy.start()
        copies.append(copy)
        if index == blocks // 2:
            coeff[...] = times(table_power, second_inverse).T * (1.0 / size)
            copy = pltpu.make_async_copy(coeff, coeff_hbm, out_sem.at[blocks])
            copy.start()
            copies.append(copy)
    for copy in copies:
        copy.wait()


def finish_call(size, mine, other, sketch, table):
    rows, n = table.shape
    k = sketch.shape[1]
    return pl.pallas_call(
        functools.partial(finish, size),
        out_shape=(jax.ShapeDtypeStruct((rows, k), F32), jax.ShapeDtypeStruct((k, n), F32)),
        in_specs=[VMEM, VMEM, VMEM, HBM],
        out_specs=(HBM, HBM),
        scratch_shapes=[
            pltpu.VMEM((rows, n), BF16),
            pltpu.VMEM((rows, k), F32),
            pltpu.VMEM((k, n), F32),
            pltpu.SemaphoreType.DMA,
            pltpu.SemaphoreType.DMA((rows // BLOCK + 1,)),
        ],
        compiler_params=PARAMS,
    )(mine, other, sketch, table)


def scatter_sum(block, axes):
    return jnp.sum(lax.all_to_all(block, axes, 0, 0), 0)


def gather(block, axes):
    count = lax.axis_size(axes)
    copies = jnp.broadcast_to(block[None], (count,) + block.shape)
    return lax.all_to_all(copies, axes, 0, 0)


def on_device(table, sketch):
    count = table.shape[0] * lax.axis_size(("x", "z", "core", "y"))
    plane = ("x", "y")
    swap = [(0, 1), (1, 0)]
    keep, send = gram_call(table)
    half = keep + lax.ppermute(send, "core", swap)
    part = scatter_sum(half.reshape(lax.axis_size(plane), -1, TILE), plane)
    part = jnp.sum(gather(part, "z"), 0)
    mine = gather(part, plane).reshape(HALF, TILE)
    other = lax.ppermute(mine, "core", swap)
    return finish_call(math.sqrt(count), mine, other, sketch, table)


def solution(mesh):
    fine = Mesh(mesh.devices.reshape(4, 8, 2, 4), ("x", "z", "core", "y"))
    split_rows = P(("x", "z", "core", "y"), None)
    return jax.shard_map(
        on_device, mesh=fine, in_specs=(split_rows, P()), out_specs=(split_rows, P()), check_vma=False
    )
```

```python
import functools
import math

import jax
import jax.numpy as jnp
from jax import lax
from jax.experimental import pallas as pl
from jax.experimental.pallas import tpu as pltpu
from jax.sharding import Mesh, PartitionSpec as P

SWEEPS = 12
NEAR = 8
BLOCK = 256
STRIP = 128
TILE = 128
PAIRS = [(i, j) for i in range(4) for j in range(i, 4)]
HALF = len(PAIRS) // 2 * TILE
F32 = jnp.float32
BF16 = jnp.bfloat16
VMEM = pl.BlockSpec(memory_space=pltpu.VMEM)
HBM = pl.BlockSpec(memory_space=pl.ANY)
PARAMS = pltpu.CompilerParams(vmem_limit_bytes=48 * 2**20)


def dot(a, b):
    return jnp.dot(a, b, preferred_element_type=F32)


def split(x):
    high = x.astype(BF16)
    return high, (x - high.astype(F32)).astype(BF16)


def product(a, b, low, strip=STRIP):
    out = []
    for start in range(0, a[0].shape[0], strip):
        rows = [part[start : start + strip] for part in a]
        both = jnp.concatenate(rows, 0)
        large = dot(both, b[0])
        sums = large[:strip]
        if len(a) == 2:
            sums = large[strip:] + sums if len(b) == 1 else sums
        if len(b) == 2:
            small = dot(both if low else rows[0], b[1])
            rest = small[:strip]
            if len(a) == 2:
                rest = rest + large[strip:]
                rest = small[strip:] + rest if low else rest
            sums = rest + sums
        out.append(sums)
    return jnp.concatenate(out, 0)


def inverse_root(gram):
    n = gram.shape[0]
    eye = lax.broadcasted_iota(jnp.int32, (n, n), 0) == lax.broadcasted_iota(jnp.int32, (n, n), 1)
    parts = split(gram)
    square = product(parts, parts, True)
    scale = jnp.sqrt(jnp.sum(gram * gram))
    factor = 0.5 / scale
    x = gram * factor
    square = (square * factor) * factor
    z = jnp.where(eye, 1.5, 0.0) - x
    x = 2.25 * x - 3.0 * square + product(split(square), split(x), False)
    for _ in range(1, NEAR):
        parts = split(x)
        square = product(parts, parts, True)
        z = 1.5 * z - product(split(z), parts, False)
        x = 2.25 * x - 3.0 * square + product(split(square), parts, False)
    e = jnp.where(eye, 0.5, 0.0) - x
    for _ in range(NEAR, SWEEPS - 1):
        parts = split(e)
        square = product(parts, parts, False)
        z = z + product(split(z), parts, False)
        e = 1.5 * square + product(split(square), parts, False)
    z = z + product(split(z), split(e), False)
    return z * (1.0 / jnp.sqrt(scale))


def gram_kernel(table_ref, keep_ref, send_ref):
    table = table_ref[...]
    k = table.shape[1] // 2

    def gram(a, b):
        return lax.dot_general(a, b, (((0,), (0,)), ((), ())), preferred_element_type=F32)

    upper = gram(table[:, :k], table)
    lower = gram(table[:, k:], table[:, k:])
    tiles = []
    for i, j in PAIRS:
        source, row, col = (upper, i, j) if i < 2 else (lower, i - 2, j - 2)
        tiles.append(source[row * TILE : (row + 1) * TILE, col * TILE : (col + 1) * TILE])
    count = len(PAIRS) // 2
    core = lax.axis_index("core")

    def store(mine, others):
        for n in range(count):
            rows = pl.ds(n * TILE, TILE)
            keep_ref[rows, :] = mine[n]
            send_ref[rows, :] = others[n]

    @pl.when(core == 0)
    def _():
        store(tiles[:count], tiles[count:])

    @pl.when(core != 0)
    def _():
        store(tiles[count:], tiles[:count])


def gram_call(table):
    half = jax.ShapeDtypeStruct((HALF, TILE), F32)
    return pl.pallas_call(
        gram_kernel,
        out_shape=(half, half),
        in_specs=[VMEM],
        out_specs=(VMEM, VMEM),
        compiler_params=PARAMS,
    )(table)


def finish(size, mine_ref, other_ref, sketch_ref, table_hbm, basis_hbm, coeff_hbm, table, basis, coeff, in_sem, out_sem):
    fetch = pltpu.make_async_copy(table_hbm, table, in_sem)
    fetch.start()
    first_core = lax.axis_index("core") == 0
    mine, other = mine_ref[...], other_ref[...]
    tiles = {}
    for n, half in enumerate((jnp.where(first_core, mine, other), jnp.where(first_core, other, mine))):
        for m in range(HALF // TILE):
            i, j = PAIRS[n * (HALF // TILE) + m]
            tile = half[m * TILE : (m + 1) * TILE, :]
            tiles[i, j] = tile
            if i != j:
                tiles[j, i] = tile.T
    total = split(jnp.concatenate([jnp.concatenate([tiles[i, j] for j in range(4)], 1) for i in range(4)], 0))
    sketch = sketch_ref[...]
    first = split(product(total, (sketch,), True))
    sketch_t = sketch.astype(F32).T.astype(BF16)
    power = product(first, split(inverse_root(product((sketch_t,), first, True))), True)
    parts = split(power)
    table_power = split(product(total, parts, True))
    second_inverse = split(inverse_root(product(split(power.T), table_power, True)))
    weight = split(product(parts, second_inverse, True) * size)
    fetch.wait()
    copies = []
    blocks = table.shape[0] // BLOCK
    for index in range(blocks):
        rows = pl.ds(index * BLOCK, BLOCK)
        basis[rows, :] = product((table[rows, :],), weight, True, BLOCK)
        copy = pltpu.make_async_copy(basis.at[rows], basis_hbm.at[rows], out_sem.at[index])
        copy.start()
        copies.append(copy)
        if index == 0:
            coeff[...] = product(table_power, second_inverse, True).T * (1.0 / size)
            copy = pltpu.make_async_copy(coeff, coeff_hbm, out_sem.at[blocks])
            copy.start()
            copies.append(copy)
    for copy in copies:
        copy.wait()


def finish_call(size, mine, other, sketch, table):
    rows, n = table.shape
    k = sketch.shape[1]
    return pl.pallas_call(
        functools.partial(finish, size),
        out_shape=(jax.ShapeDtypeStruct((rows, k), F32), jax.ShapeDtypeStruct((k, n), F32)),
        in_specs=[VMEM, VMEM, VMEM, HBM],
        out_specs=(HBM, HBM),
        scratch_shapes=[
            pltpu.VMEM((rows, n), BF16),
            pltpu.VMEM((rows, k), F32),
            pltpu.VMEM((k, n), F32),
            pltpu.SemaphoreType.DMA,
            pltpu.SemaphoreType.DMA((rows // BLOCK + 1,)),
        ],
        compiler_params=PARAMS,
    )(mine, other, sketch, table)


def scatter_sum(block, axes):
    return jnp.sum(lax.all_to_all(block, axes, 0, 0), 0)


def gather(block, axes):
    count = lax.axis_size(axes)
    copies = jnp.broadcast_to(block[None], (count,) + block.shape)
    return lax.all_to_all(copies, axes, 0, 0)


def on_device(table, sketch):
    count = table.shape[0] * lax.axis_size(("x", "z", "core", "y"))
    plane = ("x", "y")
    swap = [(0, 1), (1, 0)]
    keep, send = gram_call(table)
    half = keep + lax.ppermute(send, "core", swap)
    part = scatter_sum(half.reshape(lax.axis_size(plane), -1, TILE), plane)
    part = jnp.sum(gather(part, "z"), 0)
    mine = gather(part, plane).reshape(HALF, TILE)
    other = lax.ppermute(mine, "core", swap)
    return finish_call(math.sqrt(count), mine, other, sketch, table)


def solution(mesh):
    fine = Mesh(mesh.devices.reshape(4, 8, 2, 4), ("x", "z", "core", "y"))
    split_rows = P(("x", "z", "core", "y"), None)
    return jax.shard_map(
        on_device, mesh=fine, in_specs=(split_rows, P()), out_specs=(split_rows, P()), check_vma=False
    )
```

```python
import functools
import math

import jax
import jax.numpy as jnp
from jax import lax
from jax.experimental import pallas as pl
from jax.experimental.pallas import tpu as pltpu
from jax.sharding import Mesh, PartitionSpec as P

SWEEPS = 12
NEAR = 8
BLOCK = 256
STRIP = 128
TILE = 128
PAIRS = [(i, j) for i in range(4) for j in range(i, 4)]
HALF = len(PAIRS) // 2 * TILE
F32 = jnp.float32
BF16 = jnp.bfloat16
VMEM = pl.BlockSpec(memory_space=pltpu.VMEM)
HBM = pl.BlockSpec(memory_space=pl.ANY)
PARAMS = pltpu.CompilerParams(vmem_limit_bytes=48 * 2**20)


def dot(a, b):
    return jnp.dot(a, b, preferred_element_type=F32)


def split(x):
    high = x.astype(BF16)
    return high, (x - high.astype(F32)).astype(BF16)


def product(a, b, low, strip=STRIP):
    out = []
    for start in range(0, a[0].shape[0], strip):
        rows = [part[start : start + strip] for part in a]
        both = jnp.concatenate(rows, 0)
        large = dot(both, b[0])
        sums = large[:strip]
        if len(a) == 2:
            sums = large[strip:] + sums if len(b) == 1 else sums
        if len(b) == 2:
            small = dot(both if low else rows[0], b[1])
            rest = small[:strip]
            if len(a) == 2:
                rest = rest + large[strip:]
                rest = small[strip:] + rest if low else rest
            sums = rest + sums
        out.append(sums)
    return jnp.concatenate(out, 0)


def root_factors(gram):
    n = gram.shape[0]
    eye = lax.broadcasted_iota(jnp.int32, (n, n), 0) == lax.broadcasted_iota(jnp.int32, (n, n), 1)
    parts = split(gram)
    square = product(parts, parts, True)
    scale = jnp.sqrt(jnp.sum(gram * gram))
    factor = 0.5 / scale
    x = gram * factor
    square = (square * factor) * factor
    z = jnp.where(eye, 1.5, 0.0) - x
    x = 2.25 * x - 3.0 * square + product(split(square), split(x), False)
    for _ in range(1, NEAR):
        parts = split(x)
        square = product(parts, parts, True)
        z = 1.5 * z - product(split(z), parts, False)
        x = 2.25 * x - 3.0 * square + product(split(square), parts, False)
    e = jnp.where(eye, 0.5, 0.0) - x
    for _ in range(NEAR, SWEEPS - 1):
        parts = split(e)
        square = product(parts, parts, False)
        z = z + product(split(z), parts, False)
        e = 1.5 * square + product(split(square), parts, False)
    return z * (1.0 / jnp.sqrt(scale)), e


def last_sweep(a, parts):
    return a + product(split(a), parts, False)


def half_gram_kernel(mine, table_ref, half_ref):
    core = lax.axis_index("core")

    def tiles(*blocks):
        row = 0
        for rows, cols in blocks:
            gram = lax.dot_general(
                table_ref[:, rows], table_ref[:, cols], (((0,), (0,)), ((), ())), preferred_element_type=F32
            )
            for i in range(0, gram.shape[0], TILE):
                for j in range(0, gram.shape[1], TILE):
                    half_ref[row : row + TILE, :] = gram[i : i + TILE, j : j + TILE]
                    row += TILE

    def cols(first, last):
        return slice(first * TILE, last * TILE)

    @pl.when((core == 0) == mine)
    def _():
        tiles((cols(0, 1), cols(0, 4)), (cols(1, 2), cols(1, 2)))

    @pl.when((core == 0) != mine)
    def _():
        tiles((cols(1, 3), cols(2, 4)), (cols(3, 4), cols(3, 4)))


def half_gram(table, mine):
    return pl.pallas_call(
        functools.partial(half_gram_kernel, mine),
        out_shape=jax.ShapeDtypeStruct((HALF, TILE), F32),
        in_specs=[VMEM],
        out_specs=VMEM,
        compiler_params=PARAMS,
    )(table)


def finish(size, mine_ref, other_ref, sketch_ref, table_hbm, basis_hbm, coeff_hbm, table, basis, coeff, in_sem, out_sem):
    fetch = pltpu.make_async_copy(table_hbm, table, in_sem)
    fetch.start()
    first_core = lax.axis_index("core") == 0
    mine, other = mine_ref[...], other_ref[...]
    tiles = {}
    for n, half in enumerate((jnp.where(first_core, mine, other), jnp.where(first_core, other, mine))):
        for m in range(HALF // TILE):
            i, j = PAIRS[n * (HALF // TILE) + m]
            tile = half[m * TILE : (m + 1) * TILE, :]
            tiles[i, j] = tile
            if i != j:
                tiles[j, i] = tile.T
    total = split(jnp.concatenate([jnp.concatenate([tiles[i, j] for j in range(4)], 1) for i in range(4)], 0))
    sketch = sketch_ref[...]
    first = split(product(total, (sketch,), True))
    sketch_t = sketch.astype(F32).T.astype(BF16)
    z, e = root_factors(product((sketch_t,), first, True))
    power = last_sweep(product(first, split(z), True), split(e))
    parts = split(power)
    table_power = split(product(total, parts, True))
    z, e = root_factors(product(split(power.T), table_power, True))
    z_parts, e_parts = split(z), split(e)
    weight = split(last_sweep(product(parts, z_parts, True), e_parts) * size)
    second_inverse = split(z + product(z_parts, e_parts, False))
    fetch.wait()
    copies = []
    blocks = table.shape[0] // BLOCK
    for index in range(blocks):
        rows = pl.ds(index * BLOCK, BLOCK)
        basis[rows, :] = product((table[rows, :],), weight, True, BLOCK)
        copy = pltpu.make_async_copy(basis.at[rows], basis_hbm.at[rows], out_sem.at[index])
        copy.start()
        copies.append(copy)
        if index == 1:
            coeff[...] = product(table_power, second_inverse, True).T * (1.0 / size)
            copy = pltpu.make_async_copy(coeff, coeff_hbm, out_sem.at[blocks])
            copy.start()
            copies.append(copy)
    for copy in copies:
        copy.wait()


def finish_call(size, mine, other, sketch, table):
    rows, n = table.shape
    k = sketch.shape[1]
    return pl.pallas_call(
        functools.partial(finish, size),
        out_shape=(jax.ShapeDtypeStruct((rows, k), F32), jax.ShapeDtypeStruct((k, n), F32)),
        in_specs=[VMEM, VMEM, VMEM, HBM],
        out_specs=(HBM, HBM),
        scratch_shapes=[
            pltpu.VMEM((rows, n), BF16),
            pltpu.VMEM((rows, k), F32),
            pltpu.VMEM((k, n), F32),
            pltpu.SemaphoreType.DMA,
            pltpu.SemaphoreType.DMA((rows // BLOCK + 1,)),
        ],
        compiler_params=PARAMS,
    )(mine, other, sketch, table)


def scatter_sum(block, axes):
    return jnp.sum(lax.all_to_all(block, axes, 0, 0), 0)


def gather(block, axes):
    count = lax.axis_size(axes)
    copies = jnp.broadcast_to(block[None], (count,) + block.shape)
    return lax.all_to_all(copies, axes, 0, 0)


def on_device(table, sketch):
    count = table.shape[0] * lax.axis_size(("x", "z", "core", "y"))
    plane = ("x", "y")
    swap = [(0, 1), (1, 0)]
    sent = lax.ppermute(half_gram(table, False), "core", swap)
    half = half_gram(table, True) + sent
    part = scatter_sum(half.reshape(lax.axis_size(plane), -1, TILE), plane)
    part = jnp.sum(gather(part, "z"), 0)
    mine = gather(part, plane).reshape(HALF, TILE)
    other = lax.ppermute(mine, "core", swap)
    return finish_call(math.sqrt(count), mine, other, sketch, table)


def solution(mesh):
    fine = Mesh(mesh.devices.reshape(4, 8, 2, 4), ("x", "z", "core", "y"))
    split_rows = P(("x", "z", "core", "y"), None)
    return jax.shard_map(
        on_device, mesh=fine, in_specs=(split_rows, P()), out_specs=(split_rows, P()), check_vma=False
    )
```

```python
import functools
import math

import jax
import jax.numpy as jnp
from jax import lax
from jax.experimental import pallas as pl
from jax.experimental.pallas import tpu as pltpu
from jax.sharding import Mesh, PartitionSpec as P

SWEEPS = 12
NEAR = 8
BLOCK = 256
STRIP = 128
TILE = 128
PAIRS = [(i, j) for i in range(4) for j in range(i, 4)]
HALF = len(PAIRS) // 2 * TILE
F32 = jnp.float32
BF16 = jnp.bfloat16
VMEM = pl.BlockSpec(memory_space=pltpu.VMEM)
HBM = pl.BlockSpec(memory_space=pl.ANY)
PARAMS = pltpu.CompilerParams(vmem_limit_bytes=48 * 2**20)


def dot(a, b):
    return jnp.dot(a, b, preferred_element_type=F32)


def split(x):
    high = x.astype(BF16)
    return high, (x - high.astype(F32)).astype(BF16)


def product(a, b, low, strip=STRIP):
    out = []
    for start in range(0, a[0].shape[0], strip):
        rows = [part[start : start + strip] for part in a]
        both = jnp.concatenate(rows, 0)
        large = dot(both, b[0])
        sums = large[:strip]
        if len(a) == 2:
            sums = large[strip:] + sums if len(b) == 1 else sums
        if len(b) == 2:
            small = dot(both if low else rows[0], b[1])
            rest = small[:strip]
            if len(a) == 2:
                rest = rest + large[strip:]
                rest = small[strip:] + rest if low else rest
            sums = rest + sums
        out.append(sums)
    return jnp.concatenate(out, 0)


def root_factors(gram):
    n = gram.shape[0]
    eye = lax.broadcasted_iota(jnp.int32, (n, n), 0) == lax.broadcasted_iota(jnp.int32, (n, n), 1)
    parts = split(gram)
    square = product(parts, parts, True)
    scale = jnp.sqrt(jnp.sum(gram * gram))
    factor = 0.5 / scale
    x = gram * factor
    square = (square * factor) * factor
    z = jnp.where(eye, 1.5, 0.0) - x
    x = 2.25 * x - 3.0 * square + product(split(square), split(x), False)
    for _ in range(1, NEAR):
        parts = split(x)
        square = product(parts, parts, True)
        z = 1.5 * z - product(split(z), parts, False)
        x = 2.25 * x - 3.0 * square + product(split(square), parts, False)
    e = jnp.where(eye, 0.5, 0.0) - x
    for _ in range(NEAR, SWEEPS - 1):
        parts = split(e)
        square = product(parts, parts, False)
        z = z + product(split(z), parts, False)
        e = 1.5 * square + product(split(square), parts, False)
    return z * (1.0 / jnp.sqrt(scale)), e


def last_sweep(a, parts):
    return a + product(split(a), parts, False)


def half_gram_kernel(mine, table_ref, half_ref):
    core = lax.axis_index("core")

    def tiles(*blocks):
        row = 0
        for rows, cols in blocks:
            gram = lax.dot_general(
                table_ref[:, rows], table_ref[:, cols], (((0,), (0,)), ((), ())), preferred_element_type=F32
            )
            for i in range(0, gram.shape[0], TILE):
                for j in range(0, gram.shape[1], TILE):
                    half_ref[row : row + TILE, :] = gram[i : i + TILE, j : j + TILE]
                    row += TILE

    def cols(first, last):
        return slice(first * TILE, last * TILE)

    @pl.when((core == 0) == mine)
    def _():
        tiles((cols(0, 1), cols(0, 4)), (cols(1, 2), cols(1, 2)))

    @pl.when((core == 0) != mine)
    def _():
        tiles((cols(1, 3), cols(2, 4)), (cols(3, 4), cols(3, 4)))


def half_gram(table, mine):
    return pl.pallas_call(
        functools.partial(half_gram_kernel, mine),
        out_shape=jax.ShapeDtypeStruct((HALF, TILE), F32),
        in_specs=[VMEM],
        out_specs=VMEM,
        compiler_params=PARAMS,
    )(table)


def finish(size, mine_ref, other_ref, sketch_ref, table_hbm, basis_hbm, coeff_hbm, table, basis, coeff, in_sem, out_sem):
    fetch = pltpu.make_async_copy(table_hbm, table, in_sem)
    fetch.start()
    first_core = lax.axis_index("core") == 0
    mine, other = mine_ref[...], other_ref[...]
    tiles = {}
    for n, half in enumerate((jnp.where(first_core, mine, other), jnp.where(first_core, other, mine))):
        for m in range(HALF // TILE):
            i, j = PAIRS[n * (HALF // TILE) + m]
            tile = half[m * TILE : (m + 1) * TILE, :]
            tiles[i, j] = tile
            if i != j:
                tiles[j, i] = tile.T
    total = split(jnp.concatenate([jnp.concatenate([tiles[i, j] for j in range(4)], 1) for i in range(4)], 0))
    sketch = sketch_ref[...]
    first = split(product(total, (sketch,), True))
    sketch_t = sketch.astype(F32).T.astype(BF16)
    z, e = root_factors(product((sketch_t,), first, True))
    power = last_sweep(product(first, split(z), True), split(e))
    parts = split(power)
    table_power = split(product(total, parts, True))
    z, e = root_factors(product(split(power.T), table_power, True))
    z_parts, e_parts = split(z), split(e)
    weight = split(last_sweep(product(parts, z_parts, True), e_parts) * size)
    second_inverse = split(z + product(z_parts, e_parts, False))
    fetch.wait()
    copies = []
    blocks = table.shape[0] // BLOCK
    for index in range(blocks):
        rows = pl.ds(index * BLOCK, BLOCK)
        basis[rows, :] = product((table[rows, :],), weight, True, BLOCK)
        copy = pltpu.make_async_copy(basis.at[rows], basis_hbm.at[rows], out_sem.at[index])
        copy.start()
        copies.append(copy)
        if index == 1:
            coeff[...] = product(table_power, second_inverse, True).T * (1.0 / size)
            copy = pltpu.make_async_copy(coeff, coeff_hbm, out_sem.at[blocks])
            copy.start()
            copies.append(copy)
    for copy in copies:
        copy.wait()


def finish_call(size, mine, other, sketch, table):
    rows, n = table.shape
    k = sketch.shape[1]
    return pl.pallas_call(
        functools.partial(finish, size),
        out_shape=(jax.ShapeDtypeStruct((rows, k), F32), jax.ShapeDtypeStruct((k, n), F32)),
        in_specs=[VMEM, VMEM, VMEM, HBM],
        out_specs=(HBM, HBM),
        scratch_shapes=[
            pltpu.VMEM((rows, n), BF16),
            pltpu.VMEM((rows, k), F32),
            pltpu.VMEM((k, n), F32),
            pltpu.SemaphoreType.DMA,
            pltpu.SemaphoreType.DMA((rows // BLOCK + 1,)),
        ],
        compiler_params=PARAMS,
    )(mine, other, sketch, table)


def scatter_sum(block, axes):
    return jnp.sum(lax.all_to_all(block, axes, 0, 0), 0)


def gather(block, axes):
    count = lax.axis_size(axes)
    copies = jnp.broadcast_to(block[None], (count,) + block.shape)
    return lax.all_to_all(copies, axes, 0, 0)


def on_device(table, sketch):
    count = table.shape[0] * lax.axis_size(("x", "z", "core", "y"))
    plane = ("x", "y")
    swap = [(0, 1), (1, 0)]
    sent = lax.ppermute(half_gram(table, False), "core", swap)
    half = half_gram(table, True) + sent
    part = scatter_sum(half.reshape(lax.axis_size(plane), -1, TILE), plane)
    for apart in (4, 1, 2):
        part = part + lax.ppermute(part, "z", [(i, i ^ apart) for i in range(lax.axis_size("z"))])
    mine = gather(part, plane).reshape(HALF, TILE)
    other = lax.ppermute(mine, "core", swap)
    return finish_call(math.sqrt(count), mine, other, sketch, table)


def solution(mesh):
    fine = Mesh(mesh.devices.reshape(4, 8, 2, 4), ("x", "z", "core", "y"))
    split_rows = P(("x", "z", "core", "y"), None)
    return jax.shard_map(
        on_device, mesh=fine, in_specs=(split_rows, P()), out_specs=(split_rows, P()), check_vma=False
    )
```

```python
import functools
import math

import jax
import jax.numpy as jnp
from jax import lax
from jax.experimental import pallas as pl
from jax.experimental.pallas import tpu as pltpu
from jax.sharding import Mesh, PartitionSpec as P

SWEEPS = 12
NEAR = 8
BLOCK = 256
STRIP = 128
TILE = 128
PAIRS = [(i, j) for i in range(4) for j in range(i, 4)]
HALF = len(PAIRS) // 2 * TILE
F32 = jnp.float32
BF16 = jnp.bfloat16
VMEM = pl.BlockSpec(memory_space=pltpu.VMEM)
HBM = pl.BlockSpec(memory_space=pl.ANY)
PARAMS = pltpu.CompilerParams(vmem_limit_bytes=48 * 2**20)


def dot(a, b):
    return jnp.dot(a, b, preferred_element_type=F32)


def split(x):
    high = x.astype(BF16)
    return high, (x - high.astype(F32)).astype(BF16)


def product(a, b, low, strip=STRIP):
    out = []
    for start in range(0, a[0].shape[0], strip):
        rows = [part[start : start + strip] for part in a]
        both = jnp.concatenate(rows, 0)
        large = dot(both, b[0])
        sums = large[:strip]
        if len(a) == 2:
            sums = large[strip:] + sums if len(b) == 1 else sums
        if len(b) == 2:
            small = dot(both if low else rows[0], b[1])
            rest = small[:strip]
            if len(a) == 2:
                rest = rest + large[strip:]
                rest = small[strip:] + rest if low else rest
            sums = rest + sums
        out.append(sums)
    return jnp.concatenate(out, 0)


def root_factors(gram):
    n = gram.shape[0]
    eye = lax.broadcasted_iota(jnp.int32, (n, n), 0) == lax.broadcasted_iota(jnp.int32, (n, n), 1)
    parts = split(gram)
    square = product(parts, parts, True)
    scale = jnp.sqrt(jnp.sum(gram * gram))
    factor = 0.5 / scale
    x = gram * factor
    square = (square * factor) * factor
    z = jnp.where(eye, 1.5, 0.0) - x
    x = 2.25 * x - 3.0 * square + product(split(square), split(x), False)
    for _ in range(1, NEAR):
        parts = split(x)
        square = product(parts, parts, True)
        z = 1.5 * z - product(split(z), parts, False)
        x = 2.25 * x - 3.0 * square + product(split(square), parts, False)
    e = jnp.where(eye, 0.5, 0.0) - x
    for _ in range(NEAR, SWEEPS - 1):
        parts = split(e)
        square = product(parts, parts, False)
        z = z + product(split(z), parts, False)
        e = 1.5 * square + product(split(square), parts, False)
    return z * (1.0 / jnp.sqrt(scale)), e


def last_sweep(a, parts):
    return a + product(split(a), parts, False)


def half_gram_kernel(mine, table_ref, half_ref):
    core = lax.axis_index("core")

    def tiles(*blocks):
        row = 0
        for rows, cols in blocks:
            gram = lax.dot_general(
                table_ref[:, rows], table_ref[:, cols], (((0,), (0,)), ((), ())), preferred_element_type=F32
            )
            for i in range(0, gram.shape[0], TILE):
                for j in range(0, gram.shape[1], TILE):
                    half_ref[row : row + TILE, :] = gram[i : i + TILE, j : j + TILE]
                    row += TILE

    def cols(first, last):
        return slice(first * TILE, last * TILE)

    @pl.when((core == 0) == mine)
    def _():
        tiles((cols(0, 1), cols(0, 4)), (cols(1, 2), cols(1, 2)))

    @pl.when((core == 0) != mine)
    def _():
        tiles((cols(1, 3), cols(2, 4)), (cols(3, 4), cols(3, 4)))


def half_gram(table, mine):
    return pl.pallas_call(
        functools.partial(half_gram_kernel, mine),
        out_shape=jax.ShapeDtypeStruct((HALF, TILE), F32),
        in_specs=[VMEM],
        out_specs=VMEM,
        compiler_params=PARAMS,
    )(table)


def finish(size, mine_ref, other_ref, sketch_ref, table, basis_hbm, coeff_hbm, basis, coeff, out_sem):
    first_core = lax.axis_index("core") == 0
    mine, other = mine_ref[...], other_ref[...]
    tiles = {}
    for n, half in enumerate((jnp.where(first_core, mine, other), jnp.where(first_core, other, mine))):
        for m in range(HALF // TILE):
            i, j = PAIRS[n * (HALF // TILE) + m]
            tile = half[m * TILE : (m + 1) * TILE, :]
            tiles[i, j] = tile
            if i != j:
                tiles[j, i] = tile.T
    total = split(jnp.concatenate([jnp.concatenate([tiles[i, j] for j in range(4)], 1) for i in range(4)], 0))
    sketch = sketch_ref[...]
    first = split(product(total, (sketch,), True))
    sketch_t = sketch.astype(F32).T.astype(BF16)
    z, e = root_factors(product((sketch_t,), first, True))
    power = last_sweep(product(first, split(z), True), split(e))
    parts = split(power)
    table_power = split(product(total, parts, True))
    z, e = root_factors(product(split(power.T), table_power, True))
    z_parts, e_parts = split(z), split(e)
    weight = split(last_sweep(product(parts, z_parts, True), e_parts) * size)
    second_inverse = split(z + product(z_parts, e_parts, False))
    copies = []
    blocks = table.shape[0] // BLOCK
    for index in range(blocks):
        rows = pl.ds(index * BLOCK, BLOCK)
        basis[rows, :] = product((table[rows, :],), weight, True, BLOCK)
        copy = pltpu.make_async_copy(basis.at[rows], basis_hbm.at[rows], out_sem.at[index])
        copy.start()
        copies.append(copy)
        if index == 1:
            coeff[...] = product(table_power, second_inverse, True).T * (1.0 / size)
            copy = pltpu.make_async_copy(coeff, coeff_hbm, out_sem.at[blocks])
            copy.start()
            copies.append(copy)
    for copy in copies:
        copy.wait()


def finish_call(size, mine, other, sketch, table):
    rows, n = table.shape
    k = sketch.shape[1]
    return pl.pallas_call(
        functools.partial(finish, size),
        out_shape=(jax.ShapeDtypeStruct((rows, k), F32), jax.ShapeDtypeStruct((k, n), F32)),
        in_specs=[VMEM, VMEM, VMEM, VMEM],
        out_specs=(HBM, HBM),
        scratch_shapes=[
            pltpu.VMEM((rows, k), F32),
            pltpu.VMEM((k, n), F32),
            pltpu.SemaphoreType.DMA((rows // BLOCK + 1,)),
        ],
        compiler_params=PARAMS,
    )(mine, other, sketch, table)


def scatter_sum(block, axes):
    return jnp.sum(lax.all_to_all(block, axes, 0, 0), 0)


def gather(block, axes):
    count = lax.axis_size(axes)
    copies = jnp.broadcast_to(block[None], (count,) + block.shape)
    return lax.all_to_all(copies, axes, 0, 0)


def on_device(table, sketch):
    count = table.shape[0] * lax.axis_size(("x", "z", "core", "y"))
    plane = ("x", "y")
    swap = [(0, 1), (1, 0)]
    sent = lax.ppermute(half_gram(table, False), "core", swap)
    half = half_gram(table, True) + sent
    part = scatter_sum(half.reshape(lax.axis_size(plane), -1, TILE), plane)
    for apart in (4, 1, 2):
        part = part + lax.ppermute(part, "z", [(i, i ^ apart) for i in range(lax.axis_size("z"))])
    mine = gather(part, plane).reshape(HALF, TILE)
    other = lax.ppermute(mine, "core", swap)
    return finish_call(math.sqrt(count), mine, other, sketch, table)


def solution(mesh):
    fine = Mesh(mesh.devices.reshape(4, 8, 2, 4), ("x", "z", "core", "y"))
    split_rows = P(("x", "z", "core", "y"), None)
    return jax.shard_map(
        on_device, mesh=fine, in_specs=(split_rows, P()), out_specs=(split_rows, P()), check_vma=False
    )
```
